32 devices in a mesh: groups: 2 (over y), seq: 4 (over z), strand: 2 (over core), chan: 2 (over x).
Axes of the slice: x: 2, y: 2, z: 4, core: 2. Of those that a mesh axis runs over, the one named last changes fastest.
Arguments:
- seq_in: bfloat16 [2, 6144, 512], P('strand', ('groups', 'seq', 'chan')), parts along dimension 1, may hold values from -6 to 6
- conv_norm: float32 [2, 512], replicated, may hold values from 0.1 to 1.9
- conv_weight: bfloat16 [2, 3, 512, 512], P(None, None, None, ('seq', 'chan')), may hold values from -0.15625 to 0.15625
- ff_norm: float32 [2, 512], replicated, may hold values from 0.1 to 1.9
- up_weight: bfloat16 [2, 512, 2048], P(None, None, ('seq', 'chan')), may hold values from -0.25 to 0.25
- down_weight: bfloat16 [2, 2048, 512], P(None, ('seq', 'chan')), may hold values from -0.125 to 0.125
- head_norm: float32 [512], replicated, may hold values from 0.1 to 1.9
- value_weight: bfloat16 [512, 512], replicated, may hold values from -0.25 to 0.25
- gate_weight: bfloat16 [512, 512], replicated, may hold values from -0.25 to 0.25
- out_weight: bfloat16 [512, 512], replicated, may hold values from -0.25 to 0.25
Outputs:
- strand_out: bfloat16 [2, 6144, 512], P('strand', ('groups', 'seq', 'chan')), parts along dimension 1
The draws below stay inside these ranges and needn't reach their ends.
There are 2 independent parts, one for each index of `groups`. The reference program is written for one: setup_inputs(seed, part) draws one part's arguments, and reference() takes and returns one part's arrays. A program takes and returns all parts, laid end to end along the dimension named above; an argument that names none is the same for every part. Nothing has to cross between parts.
All inputs are finite; a program needn't handle non-finite values.
Results may differ from the reference program's by a relative error of at most 0.015.
Values may be sent and summed in bfloat16 or wider, within the bound.
A program may use at most 64 MiB of HBM per device.

```python
import jax
import jax.numpy as jnp
from jax import lax

D = 512
FF = 2048
POS_DEV = 384
BLOCKS = 2
POSITIONS = 3072
N_SEQ = 4
N_CHAN = 2


def shard_levels(key, shape, pieces, smallest, largest):
    level, own = 1.0, jax.random.fold_in(key, 6)
    for position, parts in pieces:
        draws = jnp.exp(jax.random.uniform(jax.random.fold_in(own, position), (parts,), jnp.float32, smallest / len(pieces), largest / len(pieces)))
        level = level * jnp.repeat(draws, shape[position] // parts).reshape([-1 if axis == position else 1 for axis in range(len(shape))])
    return level


def noise(rng, shape, width, most, split=(), kind=jnp.bfloat16):
    level = shard_levels(rng, shape, split, -0.22, 0.18) if split else 1.0
    array = jax.random.normal(rng, shape, jnp.float32) * width * level
    return jnp.minimum(jnp.maximum(array, -most), most).astype(kind)


def setup_inputs(seed: int = 0, part: int = 0) -> dict:
    seeds = jax.random.split(jax.random.key(seed), 11)
    part_splits = jax.random.split(jax.random.fold_in(seeds[10], part), 11)
    return {
        "seq_in": noise(part_splits[0], (2, POSITIONS, D), 1.0, 6.0, ((0, 2), (1, 8))),
        "conv_norm": jnp.clip(1.0 + 0.18 * jax.random.normal(seeds[1], (BLOCKS, D), jnp.float32), 0.1, 1.9),
        "conv_weight": noise(seeds[2], (BLOCKS, 3, D, D), (3 * D) ** -0.5, 0.15625, ((3, 8),)),
        "ff_norm": jnp.clip(1.0 + 0.18 * jax.random.normal(seeds[3], (BLOCKS, D), jnp.float32), 0.1, 1.9),
        "up_weight": noise(seeds[4], (BLOCKS, D, FF), D ** -0.5, 0.25, ((2, 8),)),
        "down_weight": noise(seeds[5], (BLOCKS, FF, D), FF ** -0.5, 0.125, ((1, 8),)),
        "head_norm": jnp.clip(1.0 + 0.18 * jax.random.normal(seeds[6], (D,), jnp.float32), 0.1, 1.9),
        "value_weight": noise(seeds[7], (D, D), D ** -0.5, 0.25),
        "gate_weight": noise(seeds[8], (D, D), D ** -0.5, 0.25),
        "out_weight": noise(seeds[9], (D, D), D ** -0.5, 0.25),
    }


def normalize(values, gain):
    return values * jax.lax.rsqrt(lax.optimization_barrier(jnp.mean(values * values, axis=-1, keepdims=True)) + 1e-06) * gain

def rowdot(left, right):
    flat = left.reshape(-1, left.shape[-1])
    result = jnp.dot(flat, right, preferred_element_type=jnp.float32)
    return result.reshape(left.shape[:-1] + (right.shape[-1],))

def reference(seq_in, conv_norm, conv_weight, ff_norm, up_weight, down_weight, head_norm, value_weight, gate_weight, out_weight):
    state = seq_in.astype(jnp.float32)
    length = state.shape[1]
    for block in range(BLOCKS):
        dilation = POS_DEV * N_CHAN * min(2 ** block, N_SEQ // 2)
        normed = normalize(state, conv_norm[block]).astype(jnp.bfloat16)
        before = jnp.pad(normed, ((0, 0), (dilation, 0), (0, 0)))[:, :length]
        after = jnp.pad(normed, ((0, 0), (0, dilation), (0, 0)))[:, dilation:]
        conv = rowdot(before, conv_weight[block, 0]) + rowdot(normed, conv_weight[block, 1]) + rowdot(after, conv_weight[block, 2])
        state = state + conv.astype(jnp.bfloat16).astype(jnp.float32)
        mixed = normalize(state, ff_norm[block]).astype(jnp.bfloat16)
        hidden = jax.nn.gelu(rowdot(mixed, up_weight[block])).astype(jnp.bfloat16)
        state = state + rowdot(hidden, down_weight[block])
    final = normalize(state, head_norm).astype(jnp.bfloat16)
    value = rowdot(final, value_weight)
    logits = rowdot(final, gate_weight).astype(jnp.bfloat16)
    mirrored = logits[::-1, ::-1]
    gated = (value * jax.nn.sigmoid(mirrored.astype(jnp.float32))).astype(jnp.bfloat16)
    return rowdot(gated, out_weight).astype(jnp.bfloat16)
```

```python
import functools

import jax
import jax.numpy as jnp
from jax import lax
from jax.experimental import pallas as pl
from jax.experimental.pallas import tpu as pltpu
from jax.sharding import PartitionSpec as P


def passed_along(value, axis, steps):
    count = lax.axis_size(axis)
    initial, last = (max(0, -steps), min(count, count - steps))
    return lax.ppermute(value, axis, [(source, source + steps) for source in range(initial, last)])


def swapped(x, axis, stride):
    return lax.ppermute(x, axis, [(i, i ^ 1 << stride) for i in range(lax.axis_size(axis))])


def normalize(values, gain):
    return values * lax.rsqrt(jnp.mean(values * values, axis=-1, keepdims=True) + 1e-06) * gain


def matmul(left, right):
    return jnp.dot(left, right, preferred_element_type=jnp.float32)


def local(
    seq_in,
    conv_norm,
    conv_weight,
    ff_norm,
    up_weight,
    down_weight,
    head_norm,
    value_weight,
    gate_weight,
    out_weight,
):
    state = seq_in[0].astype(jnp.float32)
    seq_count = lax.axis_size("seq")
    for block in range(conv_weight.shape[0]):
        reach = min(2**block, seq_count // 2)
        normed = normalize(state, conv_norm[block]).astype(jnp.bfloat16)
        before = passed_along(normed, "seq", reach)
        after = passed_along(normed, "seq", -reach)
        piece = lax.all_gather(conv_weight[block], ("seq", "chan"), axis=2, tiled=True)
        total = matmul(before, piece[0]) + matmul(normed, piece[1]) + matmul(after, piece[2])
        conv = total.astype(jnp.bfloat16)
        state = state + conv.astype(jnp.float32)
        mixed = normalize(state, ff_norm[block]).astype(jnp.bfloat16)
        hidden = jax.nn.gelu(
            matmul(mixed, lax.all_gather(up_weight[block], ("seq", "chan"), axis=1, tiled=True))
        ).astype(jnp.bfloat16)
        state = state + matmul(
            hidden, lax.all_gather(down_weight[block], ("seq", "chan"), axis=0, tiled=True)
        )
    final = normalize(state, head_norm).astype(jnp.bfloat16)
    value = matmul(final, value_weight)
    bit_count = (seq_count * lax.axis_size("chan")).bit_length() - 1
    opposite = swapped(final, "strand", 0)
    for digit in range(bit_count):
        opposite = swapped(opposite, ("seq", "chan"), digit)
    opposite = jnp.flip(opposite, 0)
    mirrored = matmul(opposite, gate_weight).astype(jnp.bfloat16)
    gated = (value * jax.nn.sigmoid(mirrored.astype(jnp.float32))).astype(jnp.bfloat16)
    result = matmul(gated, out_weight)
    return result.astype(jnp.bfloat16)[None]


def dot_t(left, right):
    return lax.dot_general(left, right, (((1,), (1,)), ((), ())), preferred_element_type=jnp.float32)


def fused_kernel(
    nz,
    nx,
    seq_ref,
    conv_norm,
    conv_ref,
    ff_norm,
    up_ref,
    down_ref,
    head_norm,
    value_ref,
    gate_ref,
    out_weight,
    out_ref,
    conv_all,
    up_all,
    down_all,
    state,
    acc,
    hidden,
    rows,
    final,
    opposite,
    send_sem,
    recv_sem,
    row_send,
    row_recv,
    last_send,
    last_recv,
):
    y, z, c, x = (lax.axis_index(a) for a in ("groups", "seq", "strand", "chan"))
    blocks = conv_ref.shape[0]
    owners = nz * nx
    me = z * nx + x
    count = rows.shape[2]
    mirror = {"seq": nz - 1 - z, "strand": 1 - c, "chan": nx - 1 - x}
    z_peer = [{"seq": lax.rem(z + d, nz)} for d in range(1, nz)]
    x_peer, y_peer, c_peer = {"chan": 1 - x}, {"groups": 1 - y}, {"strand": 1 - c}
    z_from = [lax.rem(z + nz - d, nz) for d in range(1, nz)]

    partners = z_peer + [x_peer, y_peer, c_peer, mirror]
    barrier = pltpu.get_barrier_semaphore()
    for peer in partners:
        pl.semaphore_signal(barrier, inc=1, device_id=peer, device_id_type=pl.DeviceIdType.MESH)

    segments = []
    for b in range(blocks):
        for kind, (whole, own) in enumerate(((conv_all, conv_ref), (up_all, up_ref), (down_all, down_ref))):
            whole[b, me] = own[b]
            segments.append((kind, b, whole.at[b]))

    def half(s, owner, core):
        ref = segments[s][2]
        size = ref.shape[1] // 2
        return ref.at[owner, pl.ds(pl.multiple_of(core * size, 16), size)]

    def quarter(s, owner, group):
        ref = segments[s][2]
        size = ref.shape[1] // 4
        return ref.at[owner, pl.ds(pl.multiple_of(c * (2 * size) + group * size, 16), size)]

    sent = []

    def copy(ref, s, slot, peer):
        return pltpu.make_async_remote_copy(
            src_ref=ref,
            dst_ref=ref,
            send_sem=send_sem.at[s, slot],
            recv_sem=recv_sem.at[s, slot],
            device_id=peer,
            device_id_type=pl.DeviceIdType.MESH,
        )

    def send(*args):
        one = copy(*args)
        one.start()
        sent.append(one)

    far = nz - 1
    at_z, at_x, at_y, at_yx, at_c, at_cx = (i * far for i in range(6))
    at_own, at_own_c = 6 * far, 6 * far + 1

    def stage_own(s):
        for d in range(far):
            send(quarter(s, me, y), s, at_z + d, z_peer[d])
        send(half(s, me, c), s, at_own, x_peer)

    def stage_z(s):
        for d in range(far):
            piece = quarter(s, z_from[d] * nx + x, y)
            copy(piece, s, at_z + d, z_peer[d]).wait_recv()
            send(piece, s, at_x + d, x_peer)
            send(piece, s, at_y + d, y_peer)

    def stage_x(s):
        piece = half(s, z * nx + 1 - x, c)
        copy(piece, s, at_own, x_peer).wait_recv()
        send(piece, s, at_own_c, c_peer)
        for d in range(far):
            piece = quarter(s, z_from[d] * nx + 1 - x, y)
            copy(piece, s, at_x + d, x_peer).wait_recv()
            send(piece, s, at_yx + d, y_peer)

    def stage_y(s):
        for d in range(far):
            for at_from, at_to, column in ((at_y, at_c, x), (at_yx, at_cx, 1 - x)):
                owner = z_from[d] * nx + column
                copy(quarter(s, owner, 1 - y), s, at_from + d, y_peer).wait_recv()
                send(half(s, owner, c), s, at_to + d, c_peer)

    def stage_c(s):
        copy(half(s, z * nx + 1 - x, 1 - c), s, at_own_c, c_peer).wait_recv()
        for d in range(far):
            for at, column in ((at_c, x), (at_cx, 1 - x)):
                copy(half(s, z_from[d] * nx + column, 1 - c), s, at + d, c_peer).wait_recv()

    def row_copy(b, way):
        reach = min(2**b, nz // 2)
        step = reach if way == 0 else -reach
        there = z + step
        back = z - step
        one = pltpu.make_async_remote_copy(
            src_ref=rows.at[b, 1],
            dst_ref=rows.at[b, 2 * way],
            send_sem=row_send.at[b, way],
            recv_sem=row_recv.at[b, way],
            device_id={"seq": lax.rem(there + nz, nz)},
            device_id_type=pl.DeviceIdType.MESH,
        )
        return one, (there >= 0) & (there < nz), (back >= 0) & (back < nz)

    def make_rows(b):
        rows[b, 1] = normalize(state[...], conv_norm[b : b + 1, :]).astype(jnp.bfloat16)
        for way in range(2):
            _, _, receives = row_copy(b, way)

            @pl.when(jnp.logical_not(receives))
            def _():
                rows[b, 2 * way] = jnp.zeros(rows.shape[2:], rows.dtype)

    def send_rows(b):
        for way in range(2):
            one, sends, _ = row_copy(b, way)

            @pl.when(sends)
            def _():
                one.start()

    def wait_rows(b):
        for way in range(2):
            one, _, receives = row_copy(b, way)

            @pl.when(receives)
            def _():
                one.wait_recv()

    def compute(s):
        kind, b, weights = segments[s]
        if kind == 0:
            wait_rows(b)
            taps = rows.shape[1]
            part = weights.shape[1] // taps
            acc[...] = jnp.zeros_like(acc)

            @pl.loop(0, taps)
            def _(t):
                piece = weights[:, pl.ds(pl.multiple_of(t * part, 16), part), :]
                acc[...] += dot_t(rows[b, t], piece.reshape(owners * part, piece.shape[-1]))

            state[...] += acc[...].astype(jnp.bfloat16).astype(jnp.float32)
            final[...] = normalize(state[...], ff_norm[b : b + 1, :]).astype(jnp.bfloat16)
        elif kind == 1:

            @pl.loop(0, owners)
            def _(o):
                hidden[o] = jax.nn.gelu(matmul(final[...], weights[o])).astype(jnp.bfloat16)

        else:

            @pl.loop(0, owners)
            def _(o):
                state[...] += matmul(hidden[o], weights[o])

            if b + 1 < blocks:
                make_rows(b + 1)
                send_rows(b + 1)

    state[...] = seq_ref[...].astype(jnp.float32)
    make_rows(0)
    pl.semaphore_wait(barrier, len(partners))
    send_rows(0)
    total = len(segments)
    for s in range(total):
        stage_own(s)
    for step in range(total + 3):
        for lag, stage in enumerate((stage_z, stage_x, stage_y, stage_c)):
            if 0 <= step - lag < total:
                stage(step - lag)
        if step >= 3:
            compute(step - 3)

    final[...] = normalize(state[...], head_norm[...]).astype(jnp.bfloat16)
    swap = pltpu.make_async_remote_copy(
        src_ref=final,
        dst_ref=opposite,
        send_sem=last_send,
        recv_sem=last_recv,
        device_id=mirror,
        device_id_type=pl.DeviceIdType.MESH,
    )
    swap.start()
    acc[...] = matmul(final[...], value_ref[...])
    place = lax.broadcasted_iota(jnp.int32, (count, count), 0) + lax.broadcasted_iota(jnp.int32, (count, count), 1)
    turn = jnp.where(place == count - 1, 1.0, 0.0).astype(jnp.bfloat16)
    for one in sent:
        one.wait_send()
    for b in range(blocks):
        for way in range(2):
            one, sends, _ = row_copy(b, way)

            @pl.when(sends)
            def _():
                one.wait_send()

    swap.wait()
    logits = matmul(opposite[...], gate_ref[...]).astype(jnp.bfloat16)
    mirrored = matmul(turn, logits)
    gated = (acc[...] * jax.nn.sigmoid(mirrored)).astype(jnp.bfloat16)
    out_ref[...] = matmul(gated, out_weight[...]).astype(jnp.bfloat16)


def fused(
    nz,
    nx,
    seq_in,
    conv_norm,
    conv_weight,
    ff_norm,
    up_weight,
    down_weight,
    head_norm,
    value_weight,
    gate_weight,
    out_weight,
):
    count, width = seq_in.shape[1:]
    blocks, taps, _, part = conv_weight.shape
    inner = up_weight.shape[2]
    owners = nz * nx
    conv = jnp.swapaxes(conv_weight, 2, 3).reshape(blocks, taps * part, width)
    slots = 6 * (nz - 1) + 2
    bf16, f32 = jnp.bfloat16, jnp.float32
    result = pl.pallas_call(
        functools.partial(fused_kernel, nz, nx),
        out_shape=jax.ShapeDtypeStruct((count, width), bf16),
        in_specs=[pl.BlockSpec(memory_space=pltpu.VMEM)] * 10,
        out_specs=pl.BlockSpec(memory_space=pltpu.VMEM),
        scratch_shapes=[
            pltpu.VMEM((blocks, owners, taps * part, width), bf16),
            pltpu.VMEM((blocks, owners, width, inner), bf16),
            pltpu.VMEM((blocks, owners, inner, width), bf16),
            pltpu.VMEM((count, width), f32),
            pltpu.VMEM((count, width), f32),
            pltpu.VMEM((owners, count, inner), bf16),
            pltpu.VMEM((blocks, 3, count, width), bf16),
            pltpu.VMEM((count, width), bf16),
            pltpu.VMEM((count, width), bf16),
            pltpu.SemaphoreType.DMA((3 * blocks, slots)),
            pltpu.SemaphoreType.DMA((3 * blocks, slots)),
            pltpu.SemaphoreType.DMA((blocks, 2)),
            pltpu.SemaphoreType.DMA((blocks, 2)),
            pltpu.SemaphoreType.DMA,
            pltpu.SemaphoreType.DMA,
        ],
        compiler_params=pltpu.CompilerParams(
            collective_id=0, has_side_effects=True, vmem_limit_bytes=40 * 2**20
        ),
    )(
        seq_in[0],
        conv_norm,
        conv,
        ff_norm,
        up_weight,
        down_weight,
        head_norm[None],
        value_weight,
        gate_weight,
        out_weight,
    )
    return result[None]


def takes_kernel(mesh, conv_shape, up_shape, seq_shape):
    sizes = dict(mesh.shape)
    if any(sizes[a] != 2 for a in ("groups", "strand", "chan")) or not 2 <= sizes["seq"] <= 8:
        return False
    shards = sizes["seq"] * sizes["chan"]
    conv_rows = conv_shape[1] * conv_shape[3] // shards
    inner = up_shape[2] // shards
    count = seq_shape[1] // (shards * sizes["groups"])
    return conv_rows % 64 == 0 and conv_shape[3] // shards % 16 == 0 and inner % 128 == 0 and count % 16 == 0


def solution(mesh):
    in_specs = (
        P("strand", ("groups", "seq", "chan"), None),
        P(),
        P(None, None, None, ("seq", "chan")),
        P(),
        P(None, None, ("seq", "chan")),
        P(None, ("seq", "chan"), None),
        P(),
        P(),
        P(),
        P(),
    )
    out_specs = P("strand", ("groups", "seq", "chan"), None)

    def run(*args):
        body = local
        if takes_kernel(mesh, args[2].shape, args[4].shape, args[0].shape):
            body = functools.partial(fused, mesh.shape["seq"], mesh.shape["chan"])
        return jax.shard_map(body, mesh=mesh, in_specs=in_specs, out_specs=out_specs, check_vma=False)(*args)

    return run
```

```python
import functools

import jax
import jax.numpy as jnp
from jax import lax
from jax.experimental import pallas as pl
from jax.experimental.pallas import tpu as pltpu
from jax.sharding import PartitionSpec as P


def passed_along(value, axis, steps):
    count = lax.axis_size(axis)
    initial, last = (max(0, -steps), min(count, count - steps))
    return lax.ppermute(value, axis, [(source, source + steps) for source in range(initial, last)])


def swapped(x, axis, stride):
    return lax.ppermute(x, axis, [(i, i ^ 1 << stride) for i in range(lax.axis_size(axis))])


def normalize(values, gain):
    return values * lax.rsqrt(jnp.mean(values * values, axis=-1, keepdims=True) + 1e-06) * gain


def matmul(left, right):
    return jnp.dot(left, right, preferred_element_type=jnp.float32)


def local(
    seq_in,
    conv_norm,
    conv_weight,
    ff_norm,
    up_weight,
    down_weight,
    head_norm,
    value_weight,
    gate_weight,
    out_weight,
):
    state = seq_in[0].astype(jnp.float32)
    seq_count = lax.axis_size("seq")
    for block in range(conv_weight.shape[0]):
        reach = min(2**block, seq_count // 2)
        normed = normalize(state, conv_norm[block]).astype(jnp.bfloat16)
        before = passed_along(normed, "seq", reach)
        after = passed_along(normed, "seq", -reach)
        piece = lax.all_gather(conv_weight[block], ("seq", "chan"), axis=2, tiled=True)
        total = matmul(before, piece[0]) + matmul(normed, piece[1]) + matmul(after, piece[2])
        conv = total.astype(jnp.bfloat16)
        state = state + conv.astype(jnp.float32)
        mixed = normalize(state, ff_norm[block]).astype(jnp.bfloat16)
        hidden = jax.nn.gelu(
            matmul(mixed, lax.all_gather(up_weight[block], ("seq", "chan"), axis=1, tiled=True))
        ).astype(jnp.bfloat16)
        state = state + matmul(
            hidden, lax.all_gather(down_weight[block], ("seq", "chan"), axis=0, tiled=True)
        )
    final = normalize(state, head_norm).astype(jnp.bfloat16)
    value = matmul(final, value_weight)
    bit_count = (seq_count * lax.axis_size("chan")).bit_length() - 1
    opposite = swapped(final, "strand", 0)
    for digit in range(bit_count):
        opposite = swapped(opposite, ("seq", "chan"), digit)
    opposite = jnp.flip(opposite, 0)
    mirrored = matmul(opposite, gate_weight).astype(jnp.bfloat16)
    gated = (value * jax.nn.sigmoid(mirrored.astype(jnp.float32))).astype(jnp.bfloat16)
    result = matmul(gated, out_weight)
    return result.astype(jnp.bfloat16)[None]


def dot_t(left, right):
    return lax.dot_general(left, right, (((1,), (1,)), ((), ())), preferred_element_type=jnp.float32)


def fused_kernel(
    nz,
    nx,
    seq_in,
    conv_norm_in,
    conv_ref,
    ff_norm_in,
    up_ref,
    down_ref,
    head_norm_in,
    value_in,
    gate_in,
    out_in,
    out_ref,
    seq_ref,
    conv_norm,
    ff_norm,
    head_norm,
    value_ref,
    gate_ref,
    out_weight,
    own_sem,
    small_sem,
    conv_all,
    up_all,
    down_all,
    state,
    acc,
    hidden,
    rows,
    final,
    opposite,
    send_sem,
    recv_sem,
    row_send,
    row_recv,
    last_send,
    last_recv,
):
    y, z, c, x = (lax.axis_index(a) for a in ("groups", "seq", "strand", "chan"))
    blocks = conv_ref.shape[0]
    owners = nz * nx
    me = z * nx + x
    count = rows.shape[2]
    mirror = {"seq": nz - 1 - z, "strand": 1 - c, "chan": nx - 1 - x}
    z_from = [lax.bitwise_xor(z, d) for d in range(1, nz)]
    z_peer = [{"seq": one} for one in z_from]
    x_peer, y_peer, c_peer = {"chan": 1 - x}, {"groups": 1 - y}, {"strand": 1 - c}

    partners = z_peer + [x_peer, y_peer, c_peer, mirror]
    barrier = pltpu.get_barrier_semaphore()
    for peer in partners:
        pl.semaphore_signal(barrier, inc=1, device_id=peer, device_id_type=pl.DeviceIdType.MESH)

    small = [
        pltpu.make_async_copy(source, target, small_sem.at[i])
        for i, (source, target) in enumerate(
            (
                (seq_in, seq_ref),
                (conv_norm_in, conv_norm),
                (ff_norm_in, ff_norm),
                (head_norm_in, head_norm),
                (value_in, value_ref),
                (gate_in, gate_ref),
                (out_in, out_weight),
            )
        )
    ]
    for one in small[:3]:
        one.start()
    segments = []
    own_copy = []
    for b in range(blocks):
        for kind, (whole, own) in enumerate(((conv_all, conv_ref), (up_all, up_ref), (down_all, down_ref))):
            segments.append((kind, b, whole.at[b], own.at[b]))
            own_copy.append(pltpu.make_async_copy(own.at[b], whole.at[b, me], own_sem.at[len(own_copy)]))
    for one in own_copy + small[3:]:
        one.start()

    def half_rows(s, core):
        size = segments[s][3].shape[0] // 2
        return pl.ds(pl.multiple_of(core * size, 16), size)

    def quarter_rows(s, group):
        size = segments[s][3].shape[0] // 4
        return pl.ds(pl.multiple_of(c * (2 * size) + group * size, 16), size)

    def half(s, owner, core):
        return segments[s][2].at[owner, half_rows(s, core)]

    def quarter(s, owner, group):
        return segments[s][2].at[owner, quarter_rows(s, group)]

    sent = []

    def copy(ref, s, slot, peer, source=None):
        return pltpu.make_async_remote_copy(
            src_ref=ref if source is None else source,
            dst_ref=ref,
            send_sem=send_sem.at[s, slot],
            recv_sem=recv_sem.at[s, slot],
            device_id=peer,
            device_id_type=pl.DeviceIdType.MESH,
        )

    def send(*args):
        one = copy(*args)
        one.start()
        sent.append(one)

    far = nz - 1
    at_z, at_x, at_y, at_yx, at_c, at_cx = (i * far for i in range(6))
    at_own, at_own_c = 6 * far, 6 * far + 1

    def stage_own(s):
        for d in range(far):
            if d == 0:
                send(half(s, me, c), s, at_z, z_peer[0], segments[s][3].at[half_rows(s, c)])
            else:
                send(quarter(s, me, y), s, at_z + d, z_peer[d], segments[s][3].at[quarter_rows(s, y)])
        send(half(s, me, c), s, at_own, x_peer, segments[s][3].at[half_rows(s, c)])

    def stage_z(s):
        for d in range(far):
            owner = z_from[d] * nx + x
            piece = quarter(s, owner, y)
            if d == 0:
                whole = half(s, owner, c)
                copy(whole, s, at_z, z_peer[0]).wait_recv()
                send(whole, s, at_c, c_peer)
            else:
                copy(piece, s, at_z + d, z_peer[d]).wait_recv()
                send(piece, s, at_y + d, y_peer)
            send(piece, s, at_x + d, x_peer)

    def stage_x(s):
        piece = half(s, z * nx + 1 - x, c)
        copy(piece, s, at_own, x_peer).wait_recv()
        send(piece, s, at_own_c, c_peer)
        for d in range(far):
            piece = quarter(s, z_from[d] * nx + 1 - x, y)
            copy(piece, s, at_x + d, x_peer).wait_recv()
            send(piece, s, at_yx + d, y_peer)

    def stage_y(s):
        for d in range(far):
            for at_from, at_to, column in ((at_y, at_c, x), (at_yx, at_cx, 1 - x)):
                if d == 0 and column is x:
                    continue
                owner = z_from[d] * nx + column
                copy(quarter(s, owner, 1 - y), s, at_from + d, y_peer).wait_recv()
                send(half(s, owner, c), s, at_to + d, c_peer)

    def stage_c(s):
        copy(half(s, z * nx + 1 - x, 1 - c), s, at_own_c, c_peer).wait_recv()
        for d in range(far):
            for at, column in ((at_c, x), (at_cx, 1 - x)):
                copy(half(s, z_from[d] * nx + column, 1 - c), s, at + d, c_peer).wait_recv()

    def row_copy(b, way):
        reach = min(2**b, nz // 2)
        step = reach if way == 0 else -reach
        there = z + step
        back = z - step
        one = pltpu.make_async_remote_copy(
            src_ref=rows.at[b, 1],
            dst_ref=rows.at[b, 2 * way],
            send_sem=row_send.at[b, way],
            recv_sem=row_recv.at[b, way],
            device_id={"seq": lax.rem(there + nz, nz)},
            device_id_type=pl.DeviceIdType.MESH,
        )
        return one, (there >= 0) & (there < nz), (back >= 0) & (back < nz)

    def make_rows(b):
        rows[b, 1] = normalize(state[...], conv_norm[b : b + 1, :]).astype(jnp.bfloat16)
        reach = min(2**b, nz // 2)
        for way, empty in ((0, z < reach), (1, z + reach >= nz)):

            @pl.when(empty)
            def _():
                rows[b, 2 * way] = jnp.zeros(rows.shape[2:], rows.dtype)

    def send_rows(b):
        for way in range(2):
            one, sends, _ = row_copy(b, way)

            @pl.when(sends)
            def _():
                one.start()

    def wait_rows(b):
        for way in range(2):
            one, _, receives = row_copy(b, way)

            @pl.when(receives)
            def _():
                one.wait_recv()

    def compute(s):
        kind, b, weights, _ = segments[s]
        own_copy[s].wait()
        if kind == 0:
            wait_rows(b)
            taps = rows.shape[1]
            part = weights.shape[1] // taps
            acc[...] = jnp.zeros_like(acc)

            @pl.loop(0, taps)
            def _(t):
                piece = weights[:, pl.ds(pl.multiple_of(t * part, 16), part), :]
                acc[...] += dot_t(rows[b, t], piece.reshape(owners * part, piece.shape[-1]))

            state[...] += acc[...].astype(jnp.bfloat16).astype(jnp.float32)
            final[...] = normalize(state[...], ff_norm[b : b + 1, :]).astype(jnp.bfloat16)
        elif kind == 1:

            @pl.loop(0, owners)
            def _(o):
                hidden[o] = jax.nn.gelu(matmul(final[...], weights[o])).astype(jnp.bfloat16)

        else:

            @pl.loop(0, owners)
            def _(o):
                state[...] += matmul(hidden[o], weights[o])

            if b + 1 < blocks:
                make_rows(b + 1)
                send_rows(b + 1)

    for one in small[:3]:
        one.wait()
    state[...] = seq_ref[...].astype(jnp.float32)
    make_rows(0)
    pl.semaphore_wait(barrier, len(partners))
    send_rows(0)
    total = len(segments)
    for s in range(2):
        stage_own(s)
    for step in range(total + 3):
        for lag, stage in ((2, stage_y), (1, stage_x), (0, stage_z), (3, stage_c)):
            if 0 <= step - lag < total:
                stage(step - lag)
            if lag == 0 and step + 2 < total:
                stage_own(step + 2)
        if step >= 3:
            for s in range(total):
                if s + 3 == step:
                    compute(s)

    for one in small[3:]:
        one.wait()
    final[...] = normalize(state[...], head_norm[...]).astype(jnp.bfloat16)
    swap = pltpu.make_async_remote_copy(
        src_ref=final,
        dst_ref=opposite,
        send_sem=last_send,
        recv_sem=last_recv,
        device_id=mirror,
        device_id_type=pl.DeviceIdType.MESH,
    )
    swap.start()
    acc[...] = matmul(final[...], value_ref[...])
    place = lax.broadcasted_iota(jnp.int32, (count, count), 0) + lax.broadcasted_iota(jnp.int32, (count, count), 1)
    turn = jnp.where(place == count - 1, 1.0, 0.0).astype(jnp.bfloat16)
    for one in sent:
        one.wait_send()
    for b in range(blocks):
        for way in range(2):
            one, sends, _ = row_copy(b, way)

            @pl.when(sends)
            def _():
                one.wait_send()

    swap.wait()
    logits = matmul(opposite[...], gate_ref[...]).astype(jnp.bfloat16)
    mirrored = matmul(turn, logits)
    gated = (acc[...] * jax.nn.sigmoid(mirrored)).astype(jnp.bfloat16)
    out_ref[...] = matmul(gated, out_weight[...]).astype(jnp.bfloat16)


def fused(
    nz,
    nx,
    seq_in,
    conv_norm,
    conv_weight,
    ff_norm,
    up_weight,
    down_weight,
    head_norm,
    value_weight,
    gate_weight,
    out_weight,
):
    count, width = seq_in.shape[1:]
    blocks, taps, _, part = conv_weight.shape
    inner = up_weight.shape[2]
    owners = nz * nx
    conv = jnp.swapaxes(conv_weight, 2, 3).reshape(blocks, taps * part, width)
    slots = 6 * (nz - 1) + 2
    bf16, f32 = jnp.bfloat16, jnp.float32
    result = pl.pallas_call(
        functools.partial(fused_kernel, nz, nx),
        out_shape=jax.ShapeDtypeStruct((count, width), bf16),
        in_specs=[pl.BlockSpec(memory_space=pltpu.HBM)] * 10,
        out_specs=pl.BlockSpec(memory_space=pltpu.VMEM),
        scratch_shapes=[
            pltpu.VMEM((count, width), bf16),
            pltpu.VMEM(conv_norm.shape, f32),
            pltpu.VMEM(ff_norm.shape, f32),
            pltpu.VMEM((1, width), f32),
            pltpu.VMEM(value_weight.shape, bf16),
            pltpu.VMEM(gate_weight.shape, bf16),
            pltpu.VMEM(out_weight.shape, bf16),
            pltpu.SemaphoreType.DMA((3 * blocks,)),
            pltpu.SemaphoreType.DMA((7,)),
            pltpu.VMEM((blocks, owners, taps * part, width), bf16),
            pltpu.VMEM((blocks, owners, width, inner), bf16),
            pltpu.VMEM((blocks, owners, inner, width), bf16),
            pltpu.VMEM((count, width), f32),
            pltpu.VMEM((count, width), f32),
            pltpu.VMEM((owners, count, inner), bf16),
            pltpu.VMEM((blocks, 3, count, width), bf16),
            pltpu.VMEM((count, width), bf16),
            pltpu.VMEM((count, width), bf16),
            pltpu.SemaphoreType.DMA((3 * blocks, slots)),
            pltpu.SemaphoreType.DMA((3 * blocks, slots)),
            pltpu.SemaphoreType.DMA((blocks, 2)),
            pltpu.SemaphoreType.DMA((blocks, 2)),
            pltpu.SemaphoreType.DMA,
            pltpu.SemaphoreType.DMA,
        ],
        compiler_params=pltpu.CompilerParams(
            collective_id=0, has_side_effects=True, vmem_limit_bytes=60 * 2**20
        ),
    )(
        seq_in[0],
        conv_norm,
        conv,
        ff_norm,
        up_weight,
        down_weight,
        head_norm[None],
        value_weight,
        gate_weight,
        out_weight,
    )
    return result[None]


def takes_kernel(mesh, conv_shape, up_shape, seq_shape):
    sizes = dict(mesh.shape)
    if any(sizes[a] != 2 for a in ("groups", "strand", "chan")) or not 2 <= sizes["seq"] <= 8:
        return False
    shards = sizes["seq"] * sizes["chan"]
    conv_rows = conv_shape[1] * conv_shape[3] // shards
    inner = up_shape[2] // shards
    count = seq_shape[1] // (shards * sizes["groups"])
    return conv_rows % 64 == 0 and conv_shape[3] // shards % 16 == 0 and inner % 128 == 0 and count % 16 == 0


def solution(mesh):
    in_specs = (
        P("strand", ("groups", "seq", "chan"), None),
        P(),
        P(None, None, None, ("seq", "chan")),
        P(),
        P(None, None, ("seq", "chan")),
        P(None, ("seq", "chan"), None),
        P(),
        P(),
        P(),
        P(),
    )
    out_specs = P("strand", ("groups", "seq", "chan"), None)

    def run(*args):
        body = local
        if takes_kernel(mesh, args[2].shape, args[4].shape, args[0].shape):
            body = functools.partial(fused, mesh.shape["seq"], mesh.shape["chan"])
        return jax.shard_map(body, mesh=mesh, in_specs=in_specs, out_specs=out_specs, check_vma=False)(*args)

    return run
```

```python
import functools

import jax
import jax.numpy as jnp
from jax import lax
from jax.experimental import pallas as pl
from jax.experimental.pallas import tpu as pltpu
from jax.sharding import PartitionSpec as P


def passed_along(value, axis, steps):
    count = lax.axis_size(axis)
    initial, last = (max(0, -steps), min(count, count - steps))
    return lax.ppermute(value, axis, [(source, source + steps) for source in range(initial, last)])


def swapped(x, axis, stride):
    return lax.ppermute(x, axis, [(i, i ^ 1 << stride) for i in range(lax.axis_size(axis))])


def normalize(values, gain):
    return values * lax.rsqrt(jnp.mean(values * values, axis=-1, keepdims=True) + 1e-06) * gain


def matmul(left, right):
    return jnp.dot(left, right, preferred_element_type=jnp.float32)


def local(
    seq_in,
    conv_norm,
    conv_weight,
    ff_norm,
    up_weight,
    down_weight,
    head_norm,
    value_weight,
    gate_weight,
    out_weight,
):
    state = seq_in[0].astype(jnp.float32)
    seq_count = lax.axis_size("seq")
    for block in range(conv_weight.shape[0]):
        reach = min(2**block, seq_count // 2)
        normed = normalize(state, conv_norm[block]).astype(jnp.bfloat16)
        before = passed_along(normed, "seq", reach)
        after = passed_along(normed, "seq", -reach)
        piece = lax.all_gather(conv_weight[block], ("seq", "chan"), axis=2, tiled=True)
        total = matmul(before, piece[0]) + matmul(normed, piece[1]) + matmul(after, piece[2])
        conv = total.astype(jnp.bfloat16)
        state = state + conv.astype(jnp.float32)
        mixed = normalize(state, ff_norm[block]).astype(jnp.bfloat16)
        hidden = jax.nn.gelu(
            matmul(mixed, lax.all_gather(up_weight[block], ("seq", "chan"), axis=1, tiled=True))
        ).astype(jnp.bfloat16)
        state = state + matmul(
            hidden, lax.all_gather(down_weight[block], ("seq", "chan"), axis=0, tiled=True)
        )
    final = normalize(state, head_norm).astype(jnp.bfloat16)
    value = matmul(final, value_weight)
    bit_count = (seq_count * lax.axis_size("chan")).bit_length() - 1
    opposite = swapped(final, "strand", 0)
    for digit in range(bit_count):
        opposite = swapped(opposite, ("seq", "chan"), digit)
    opposite = jnp.flip(opposite, 0)
    mirrored = matmul(opposite, gate_weight).astype(jnp.bfloat16)
    gated = (value * jax.nn.sigmoid(mirrored.astype(jnp.float32))).astype(jnp.bfloat16)
    result = matmul(gated, out_weight)
    return result.astype(jnp.bfloat16)[None]


def dot_t(left, right):
    return lax.dot_general(left, right, (((1,), (1,)), ((), ())), preferred_element_type=jnp.float32)


def fused_kernel(
    nz,
    nx,
    seq_in,
    conv_norm_in,
    conv_ref,
    ff_norm_in,
    up_ref,
    down_ref,
    head_norm_in,
    value_in,
    gate_in,
    out_in,
    out_ref,
    seq_ref,
    conv_norm,
    ff_norm,
    head_norm,
    value_ref,
    gate_ref,
    out_weight,
    own_sem,
    small_sem,
    conv_all,
    up_all,
    down_all,
    state,
    acc,
    hidden,
    rows,
    final,
    opposite,
    send_sem,
    recv_sem,
    row_send,
    row_recv,
    last_send,
    last_recv,
):
    y, z, c, x = (lax.axis_index(a) for a in ("groups", "seq", "strand", "chan"))
    blocks = conv_ref.shape[0]
    owners = nz * nx
    me = z * nx + x
    count = rows.shape[2]
    mirror = {"seq": nz - 1 - z, "strand": 1 - c, "chan": nx - 1 - x}
    z_from = [lax.bitwise_xor(z, d) for d in range(1, nz)]
    z_peer = [{"seq": one} for one in z_from]
    x_peer, y_peer, c_peer = {"chan": 1 - x}, {"groups": 1 - y}, {"strand": 1 - c}

    partners = z_peer + [x_peer, y_peer, c_peer, mirror]
    barrier = pltpu.get_barrier_semaphore()
    for peer in partners:
        pl.semaphore_signal(barrier, inc=1, device_id=peer, device_id_type=pl.DeviceIdType.MESH)

    small = [
        pltpu.make_async_copy(source, target, small_sem.at[i])
        for i, (source, target) in enumerate(
            (
                (seq_in, seq_ref),
                (conv_norm_in, conv_norm),
                (ff_norm_in, ff_norm),
                (head_norm_in, head_norm),
                (value_in, value_ref),
                (gate_in, gate_ref),
                (out_in, out_weight),
            )
        )
    ]
    for one in small[:3]:
        one.start()
    segments = []
    own_copy = []
    for b in range(blocks):
        for kind, (whole, own) in enumerate(((conv_all, conv_ref), (up_all, up_ref), (down_all, down_ref))):
            segments.append((kind, b, whole.at[b], own.at[b]))
            own_copy.append(pltpu.make_async_copy(own.at[b], whole.at[b, me], own_sem.at[len(own_copy)]))
    for one in own_copy + small[3:]:
        one.start()

    def half_rows(s, core):
        size = segments[s][3].shape[0] // 2
        return pl.ds(pl.multiple_of(core * size, 16), size)

    def quarter_rows(s, group):
        size = segments[s][3].shape[0] // 4
        return pl.ds(pl.multiple_of(c * (2 * size) + group * size, 16), size)

    def half(s, owner, core):
        return segments[s][2].at[owner, half_rows(s, core)]

    def quarter(s, owner, group):
        return segments[s][2].at[owner, quarter_rows(s, group)]

    sent = []

    def copy(ref, s, slot, peer, source=None):
        return pltpu.make_async_remote_copy(
            src_ref=ref if source is None else source,
            dst_ref=ref,
            send_sem=send_sem.at[s, slot],
            recv_sem=recv_sem.at[s, slot],
            device_id=peer,
            device_id_type=pl.DeviceIdType.MESH,
        )

    def send(*args):
        one = copy(*args)
        one.start()
        sent.append(one)

    far = nz - 1
    at_z, at_x, at_y, at_yx, at_c, at_cx = (i * far for i in range(6))
    at_own, at_own_c = 6 * far, 6 * far + 1

    def stage_own(s):
        for d in range(far):
            if d == 0:
                send(half(s, me, c), s, at_z, z_peer[0], segments[s][3].at[half_rows(s, c)])
            else:
                send(quarter(s, me, y), s, at_z + d, z_peer[d], segments[s][3].at[quarter_rows(s, y)])
        send(half(s, me, c), s, at_own, x_peer, segments[s][3].at[half_rows(s, c)])

    def stage_z(s):
        for d in range(far):
            owner = z_from[d] * nx + x
            piece = quarter(s, owner, y)
            if d == 0:
                whole = half(s, owner, c)
                copy(whole, s, at_z, z_peer[0]).wait_recv()
                send(whole, s, at_c, c_peer)
            else:
                copy(piece, s, at_z + d, z_peer[d]).wait_recv()
                send(piece, s, at_y + d, y_peer)
            send(piece, s, at_x + d, x_peer)

    def stage_x(s):
        piece = half(s, z * nx + 1 - x, c)
        copy(piece, s, at_own, x_peer).wait_recv()
        send(piece, s, at_own_c, c_peer)
        for d in range(far):
            piece = quarter(s, z_from[d] * nx + 1 - x, y)
            copy(piece, s, at_x + d, x_peer).wait_recv()
            send(piece, s, at_yx + d, y_peer)

    def stage_y(s):
        for d in range(far):
            for at_from, at_to, column in ((at_y, at_c, x), (at_yx, at_cx, 1 - x)):
                if d == 0 and column is x:
                    continue
                owner = z_from[d] * nx + column
                copy(quarter(s, owner, 1 - y), s, at_from + d, y_peer).wait_recv()
                send(half(s, owner, c), s, at_to + d, c_peer)

    def stage_c(s):
        copy(half(s, z * nx + 1 - x, 1 - c), s, at_own_c, c_peer).wait_recv()
        for d in range(far):
            for at, column in ((at_c, x), (at_cx, 1 - x)):
                copy(half(s, z_from[d] * nx + column, 1 - c), s, at + d, c_peer).wait_recv()

    def row_copy(b, way):
        reach = min(2**b, nz // 2)
        step = reach if way == 0 else -reach
        there = z + step
        back = z - step
        one = pltpu.make_async_remote_copy(
            src_ref=rows.at[b, 1],
            dst_ref=rows.at[b, 2 * way],
            send_sem=row_send.at[b, way],
            recv_sem=row_recv.at[b, way],
            device_id={"seq": lax.rem(there + nz, nz)},
            device_id_type=pl.DeviceIdType.MESH,
        )
        return one, (there >= 0) & (there < nz), (back >= 0) & (back < nz)

    def make_rows(b):
        rows[b, 1] = normalize(state[...], conv_norm[b : b + 1, :]).astype(jnp.bfloat16)
        reach = min(2**b, nz // 2)
        for way, empty in ((0, z < reach), (1, z + reach >= nz)):

            @pl.when(empty)
            def _():
                rows[b, 2 * way] = jnp.zeros(rows.shape[2:], rows.dtype)

    def send_rows(b):
        for way in range(2):
            one, sends, _ = row_copy(b, way)

            @pl.when(sends)
            def _():
                one.start()

    def wait_rows(b):
        for way in range(2):
            one, _, receives = row_copy(b, way)

            @pl.when(receives)
            def _():
                one.wait_recv()

    cuts = last_send.shape[0]
    cut = count // cuts
    spans = [pl.ds(i * cut, cut) for i in range(cuts)]
    swaps = [
        pltpu.make_async_remote_copy(
            src_ref=final.at[span],
            dst_ref=opposite.at[span],
            send_sem=last_send.at[i],
            recv_sem=last_recv.at[i],
            device_id=mirror,
            device_id_type=pl.DeviceIdType.MESH,
        )
        for i, span in enumerate(spans)
    ]

    def compute(s):
        kind, b, weights, _ = segments[s]
        own_copy[s].wait()
        if kind == 0:
            part = weights.shape[1] // rows.shape[1]
            piece = weights[:, part : 2 * part, :]
            acc[...] = dot_t(rows[b, 1], piece.reshape(owners * part, piece.shape[-1]))
            wait_rows(b)

            @pl.loop(0, 2)
            def _(side):
                piece = weights[:, pl.ds(pl.multiple_of(side * (2 * part), 16), part), :]
                acc[...] += dot_t(rows[b, 2 * side], piece.reshape(owners * part, piece.shape[-1]))

            state[...] += acc[...].astype(jnp.bfloat16).astype(jnp.float32)
            final[...] = normalize(state[...], ff_norm[b : b + 1, :]).astype(jnp.bfloat16)
        elif kind == 1:

            @pl.loop(0, owners)
            def _(o):
                hidden[o] = jax.nn.gelu(matmul(final[...], weights[o])).astype(jnp.bfloat16)

        elif b + 1 < blocks:

            @pl.loop(0, owners)
            def _(o):
                state[...] += matmul(hidden[o], weights[o])

            make_rows(b + 1)
            send_rows(b + 1)
        else:
            for one in small[3:]:
                one.wait()
            for i, swap in enumerate(swaps):
                span = spans[i]

                @pl.loop(0, owners)
                def _(o):
                    state[span, :] += matmul(hidden[o, span, :], weights[o])

                final[span, :] = normalize(state[span, :], head_norm[...]).astype(jnp.bfloat16)
                swap.start()

    for one in small[:3]:
        one.wait()
    state[...] = seq_ref[...].astype(jnp.float32)
    make_rows(0)
    pl.semaphore_wait(barrier, len(partners))
    send_rows(0)
    total = len(segments)
    for s in range(3):
        stage_own(s)
    for step in range(total + 3):
        for lag, stage in ((2, stage_y), (1, stage_x), (0, stage_z), (3, stage_c)):
            if 0 <= step - lag < total:
                stage(step - lag)
            if lag == 0 and step + 3 < total:
                stage_own(step + 3)
        if step >= 3:
            for s in range(total):
                if s + 3 == step:
                    compute(s)

    acc[...] = matmul(final[...], value_ref[...])
    place = lax.broadcasted_iota(jnp.int32, (cut, cut), 0) + lax.broadcasted_iota(jnp.int32, (cut, cut), 1)
    turn = jnp.where(place == cut - 1, 1.0, 0.0).astype(jnp.bfloat16)
    for one in sent:
        one.wait_send()
    for b in range(blocks):
        for way in range(2):
            one, sends, _ = row_copy(b, way)

            @pl.when(sends)
            def _():
                one.wait_send()

    for i, swap in enumerate(swaps):
        swap.wait()
        logits = matmul(opposite[spans[i], :], gate_ref[...]).astype(jnp.bfloat16)
        mirrored = matmul(turn, logits)
        span = spans[cuts - 1 - i]
        gated = (acc[span, :] * jax.nn.sigmoid(mirrored)).astype(jnp.bfloat16)
        out_ref[span, :] = matmul(gated, out_weight[...]).astype(jnp.bfloat16)


def fused(
    nz,
    nx,
    seq_in,
    conv_norm,
    conv_weight,
    ff_norm,
    up_weight,
    down_weight,
    head_norm,
    value_weight,
    gate_weight,
    out_weight,
):
    count, width = seq_in.shape[1:]
    blocks, taps, _, part = conv_weight.shape
    inner = up_weight.shape[2]
    owners = nz * nx
    conv = jnp.swapaxes(conv_weight, 2, 3).reshape(blocks, taps * part, width)
    slots = 6 * (nz - 1) + 2
    bf16, f32 = jnp.bfloat16, jnp.float32
    result = pl.pallas_call(
        functools.partial(fused_kernel, nz, nx),
        out_shape=jax.ShapeDtypeStruct((count, width), bf16),
        in_specs=[pl.BlockSpec(memory_space=pltpu.HBM)] * 10,
        out_specs=pl.BlockSpec(memory_space=pltpu.VMEM),
        scratch_shapes=[
            pltpu.VMEM((count, width), bf16),
            pltpu.VMEM(conv_norm.shape, f32),
            pltpu.VMEM(ff_norm.shape, f32),
            pltpu.VMEM((1, width), f32),
            pltpu.VMEM(value_weight.shape, bf16),
            pltpu.VMEM(gate_weight.shape, bf16),
            pltpu.VMEM(out_weight.shape, bf16),
            pltpu.SemaphoreType.DMA((3 * blocks,)),
            pltpu.SemaphoreType.DMA((7,)),
            pltpu.VMEM((blocks, owners, taps * part, width), bf16),
            pltpu.VMEM((blocks, owners, width, inner), bf16),
            pltpu.VMEM((blocks, owners, inner, width), bf16),
            pltpu.VMEM((count, width), f32),
            pltpu.VMEM((count, width), f32),
            pltpu.VMEM((owners, count, inner), bf16),
            pltpu.VMEM((blocks, 3, count, width), bf16),
            pltpu.VMEM((count, width), bf16),
            pltpu.VMEM((count, width), bf16),
            pltpu.SemaphoreType.DMA((3 * blocks, slots)),
            pltpu.SemaphoreType.DMA((3 * blocks, slots)),
            pltpu.SemaphoreType.DMA((blocks, 2)),
            pltpu.SemaphoreType.DMA((blocks, 2)),
            pltpu.SemaphoreType.DMA((3,)),
            pltpu.SemaphoreType.DMA((3,)),
        ],
        compiler_params=pltpu.CompilerParams(
            collective_id=0, has_side_effects=True, vmem_limit_bytes=60 * 2**20
        ),
    )(
        seq_in[0],
        conv_norm,
        conv,
        ff_norm,
        up_weight,
        down_weight,
        head_norm[None],
        value_weight,
        gate_weight,
        out_weight,
    )
    return result[None]


def takes_kernel(mesh, conv_shape, up_shape, seq_shape):
    sizes = dict(mesh.shape)
    if any(sizes[a] != 2 for a in ("groups", "strand", "chan")) or not 2 <= sizes["seq"] <= 8:
        return False
    shards = sizes["seq"] * sizes["chan"]
    conv_rows = conv_shape[1] * conv_shape[3] // shards
    inner = up_shape[2] // shards
    count = seq_shape[1] // (shards * sizes["groups"])
    return conv_rows % 64 == 0 and conv_shape[3] // shards % 16 == 0 and inner % 128 == 0 and count % 48 == 0


def solution(mesh):
    in_specs = (
        P("strand", ("groups", "seq", "chan"), None),
        P(),
        P(None, None, None, ("seq", "chan")),
        P(),
        P(None, None, ("seq", "chan")),
        P(None, ("seq", "chan"), None),
        P(),
        P(),
        P(),
        P(),
    )
    out_specs = P("strand", ("groups", "seq", "chan"), None)

    def run(*args):
        body = local
        if takes_kernel(mesh, args[2].shape, args[4].shape, args[0].shape):
            body = functools.partial(fused, mesh.shape["seq"], mesh.shape["chan"])
        return jax.shard_map(body, mesh=mesh, in_specs=in_specs, out_specs=out_specs, check_vma=False)(*args)

    return run
```
